32 devices in a mesh: wall: 4 (over x, core), span: 4 (over z), stream: 2 (over y).
Axes of the slice: x: 2, y: 2, z: 4, core: 2. Of those that a mesh axis runs over, the one named last changes fastest.
Arguments:
- right_side: float32 [4, 2, 8, 64, 320], P('span', 'stream', 'wall'), may hold values from -6 to 6
- old_values: float32 [4, 2, 8, 64, 320], P('span', 'stream', 'wall'), may hold values from -6 to 6
- element_library: float32 [8, 320], replicated, as said below
- wall_library: float32 [3, 320, 320], replicated, as said below
- face_library: float32 [4, 320, 320], replicated, may hold values from -0.15625 to 0.15625
- element_index: int32 [4, 2, 8], P('span', 'stream', 'wall'), may hold values from 0 to 7
- wall_faces: int32 [4, 2, 8, 2], P('span', 'stream', 'wall'), may hold values from 0 to 2, as said below
- face_index: int32 [4, 2, 8, 4], P('span', 'stream', 'wall'), may hold values from 0 to 3
Outputs:
- new_values: float32 [4, 2, 8, 64, 320], P('span', 'stream', 'wall')
The draws below stay inside these ranges and needn't reach their ends.
Inputs may be any that keep to these rules, and one draw needn't show every extreme that they name: On every line wall_faces[..., i, 1] equals wall_faces[..., i + 1, 0] for i < 7. `wall_library`: every block is symmetric positive definite. `element_library`: entries are positive.
All inputs are finite; a program needn't handle non-finite values.
Results may differ from the reference program's by a relative error of at most 0.0003.
Values sent between devices are 32-bit elements; how exact they have to be, the bound alone decides.
A program may use at most 64 MiB of HBM per device.

```python
import math
import jax
import jax.numpy as jnp
from jax import lax

ELEMENT_UNKNOWNS = 320
NVEC = 64
NQ = 3
NN = 4
LIBRARY_ELEMENTS = 8
LINE = 8
NSPAN = 4
NFLOW = 2


wall_strength = 10.0


def draw_element_library(key, part):
    key_select, key_gradual, key_quick, key_sudden, key_rows_draw = jax.random.split(key, 5)
    share = 0.5
    slow_mask = jax.random.uniform(key_select, (LIBRARY_ELEMENTS, ELEMENT_UNKNOWNS), jnp.float32) < share
    slow_rate = jnp.exp(jax.random.uniform(key_gradual, (LIBRARY_ELEMENTS, ELEMENT_UNKNOWNS), jnp.float32, math.log(0.002), math.log(0.01)))
    fast_rate = jnp.exp(jax.random.uniform(key_quick, (LIBRARY_ELEMENTS, ELEMENT_UNKNOWNS), jnp.float32, math.log(1.0), math.log(10.0)))
    sudden_rate = jnp.exp(jax.random.uniform(key_sudden, (LIBRARY_ELEMENTS, ELEMENT_UNKNOWNS), jnp.float32, math.log(0.5), math.log(1.5)))
    sudden_row = jax.random.randint(key_rows_draw, (), 0, LIBRARY_ELEMENTS, dtype=jnp.int32)
    rate_values = jnp.where(slow_mask, slow_rate, fast_rate)
    library_row_list = jnp.arange(LIBRARY_ELEMENTS, dtype=jnp.int32)[:, None]
    return jnp.where(library_row_list == sudden_row, sudden_rate, rate_values)


def draw_wall_library(key, part):
    key_noise, key_diag = jax.random.split(key)
    spread = 0.1
    reach = 0.6
    raw = jax.random.uniform(key_noise, (NQ, ELEMENT_UNKNOWNS, ELEMENT_UNKNOWNS), jnp.float32, -1.0, 1.0)
    noise = (raw + jnp.swapaxes(raw, 1, 2)) * (0.5 * reach * wall_strength / math.sqrt(ELEMENT_UNKNOWNS))
    diagonal = wall_strength * jax.random.uniform(key_diag, (NQ, ELEMENT_UNKNOWNS), jnp.float32, 1.0 - spread, 1.0 + spread)
    return noise + diagonal[:, :, None] * jnp.eye(ELEMENT_UNKNOWNS, dtype=jnp.float32)[None]


def draw_wall_faces(key, part):
    faces = jax.random.randint(key, (NSPAN, NFLOW, LINE + 1), 0, NQ, dtype=jnp.int32)
    return jnp.stack([faces[:, :, :-1], faces[:, :, 1:]], axis=-1)


def set_ends(entries, own_key, smallest, high):
    longest = entries.shape.index(max(entries.shape))
    spots = []
    for shift in (0, 1):
        where = [jax.random.randint(jax.random.fold_in(own_key, axis), (), 0, length) for axis, length in enumerate(entries.shape)]
        where[longest] = (where[longest] + shift) % entries.shape[longest]
        spots.append(tuple(where))
    return entries.at[spots[0]].set(smallest).at[spots[1]].set(high)


def level_of(own_key, dims, cuts, least, largest):
    factor_of = 1.0
    for dim, shards_of in cuts:
        heights = jax.random.uniform(jax.random.fold_in(jax.random.fold_in(own_key, 6), dim), (shards_of,), jnp.float32, least / len(cuts), largest / len(cuts))
        factor_of = factor_of * jnp.repeat(jnp.exp(heights), dims[dim] // shards_of).reshape((-1,) + (1,) * (len(dims) - 1 - dim))
    return factor_of


def normal_values(key, dims, scale, most, cuts=(), held_as=jnp.bfloat16):
    drawn = jax.random.normal(key, dims, jnp.float32) * scale
    if len(cuts) > 0:
        drawn = level_of(key, dims, cuts, -0.22, 0.18) * drawn
    return jnp.clip(drawn, min=-most, max=most).astype(held_as)


def setup_inputs(seed: int = 0) -> dict:
    arg_keys = jax.random.split(jax.random.key(seed), 9)
    right_side = normal_values(arg_keys[0], (NSPAN, NFLOW, LINE, NVEC, ELEMENT_UNKNOWNS), 1.0, 6.0, ((0, 4), (1, 2), (2, 4)), jnp.float32)
    old_values = normal_values(arg_keys[1], (NSPAN, NFLOW, LINE, NVEC, ELEMENT_UNKNOWNS), 1.0, 6.0, ((0, 4), (1, 2), (2, 4)), jnp.float32)
    element_library = draw_element_library(jax.random.fold_in(arg_keys[8], 71), 0)
    wall_library = draw_wall_library(jax.random.fold_in(arg_keys[8], 71), 0)
    face_library = normal_values(arg_keys[4], (NN, ELEMENT_UNKNOWNS, ELEMENT_UNKNOWNS), (4 * ELEMENT_UNKNOWNS) ** -0.5, 0.15625, (), jnp.float32)
    element_index = set_ends(jax.random.randint(arg_keys[5], (NSPAN, NFLOW, LINE), 0, LIBRARY_ELEMENTS), jax.random.fold_in(arg_keys[5], 1), 0, LIBRARY_ELEMENTS - 1).astype(jnp.int32)
    wall_faces = draw_wall_faces(jax.random.fold_in(arg_keys[8], 71), 0)
    face_index = set_ends(jax.random.randint(arg_keys[7], (NSPAN, NFLOW, LINE, 4), 0, NN), jax.random.fold_in(arg_keys[7], 1), 0, NN - 1).astype(jnp.int32)
    return dict(right_side=right_side, old_values=old_values, element_library=element_library, wall_library=wall_library, face_library=face_library, element_index=element_index, wall_faces=wall_faces, face_index=face_index)


HIGHEST = lax.Precision.HIGHEST

def lower_solve(factor, values):
    return jax.scipy.linalg.solve_triangular(factor, values, lower=True)

def upper_solve(factor, values):
    return jax.scipy.linalg.solve_triangular(factor, values, lower=True, trans=1)

def solve_line(residual_t, element_rates, line_faces, wall_library):

    def pivot_of(rate_row, face_pair):
        return jnp.diag(rate_row) + wall_library[face_pair[0]] + wall_library[face_pair[1]]
    first_factor = jnp.linalg.cholesky(pivot_of(element_rates[0], line_faces[0]))

    def advance_one(carried_state, per_element):
        factor_prev, carried_prev = carried_state
        rate_row, face_pair, residual_row = per_element
        coupling = wall_library[face_pair[0]]
        scaled = lower_solve(factor_prev, coupling)
        reduced = lower_solve(factor_prev, carried_prev)
        pivot_now = pivot_of(rate_row, face_pair) - jnp.dot(scaled.T, scaled, precision=HIGHEST)
        carried = residual_row + jnp.dot(scaled.T, reduced, precision=HIGHEST)
        factor = jnp.linalg.cholesky(pivot_now)
        return ((factor, carried), (factor, carried))
    start_carry = (first_factor, residual_t[0])
    unused_state, (factors, carries) = lax.scan(advance_one, start_carry, (element_rates[1:], line_faces[1:], residual_t[1:]))
    factors = jnp.concatenate([first_factor[None], factors], axis=0)
    carries = jnp.concatenate([residual_t[:1], carries], axis=0)

    def retreat_one(term_next, per_element):
        factor, carried, face_pair = per_element
        solution = upper_solve(factor, lower_solve(factor, carried + term_next))
        return (jnp.dot(wall_library[face_pair[0]], solution, precision=HIGHEST), solution)
    unused_term, solutions = lax.scan(retreat_one, jnp.zeros_like(residual_t[0]), (factors, carries, line_faces), reverse=True)
    return solutions

def reference(right_side, old_values, element_library, wall_library, face_library, element_index, wall_faces, face_index):

    def one_line(line_number):
        span_pos = line_number // NFLOW
        flow_pos = line_number % NFLOW

        def neighbour(span_at, flow_at):
            return old_values[span_at % NSPAN, flow_at % NFLOW]
        near_rows = jnp.stack([neighbour(span_pos - 1, flow_pos), neighbour(span_pos + 1, flow_pos), neighbour(span_pos, flow_pos - 1), neighbour(span_pos, flow_pos + 1)], axis=1)
        blocks = face_library[face_index[span_pos, flow_pos]]
        coupled = jnp.einsum('edjk,edvk->ejv', blocks, near_rows, precision=HIGHEST)
        residual_t = jnp.swapaxes(right_side[span_pos, flow_pos], 1, 2) - coupled
        element_rates = element_library[element_index[span_pos, flow_pos]]
        solutions = solve_line(residual_t, element_rates, wall_faces[span_pos, flow_pos], wall_library)
        return jnp.swapaxes(solutions, 1, 2)
    lines = lax.map(one_line, jnp.arange(NSPAN * NFLOW, dtype=jnp.int32))
    return lines.reshape((NSPAN, NFLOW, LINE, NVEC, ELEMENT_UNKNOWNS))
```

```python
import functools
import jax
import jax.numpy as jnp
from jax import lax
from jax.experimental import pallas as pl
from jax.experimental.pallas import tpu as pltpu
from jax.sharding import PartitionSpec as P

F32 = jnp.float32
BF16 = jnp.bfloat16
LOW_STEPS = 4
HIGH_STEPS = 4
CONVERGED = 3e-3


def dot(a, b, transposed=False):
    dims = (((1,), (1,)), ((), ())) if transposed else (((1,), (0,)), ((), ()))
    return lax.dot_general(a, b, dims, preferred_element_type=F32)


def split(a):
    high = a.astype(BF16)
    return high, (a - high.astype(F32)).astype(BF16)


def dot3(a, b, transposed=False):
    return (
        dot(a[0], b[0], transposed) + (dot(a[0], b[1], transposed) + dot(a[1], b[0], transposed))
    )


def eye_mask(size):
    row = lax.broadcasted_iota(jnp.int32, (size, size), 0)
    col = lax.broadcasted_iota(jnp.int32, (size, size), 1)
    return row == col


def gauss_jordan(a_ref, x_ref):
    size = a_ref.shape[0]
    x_ref[...] = a_ref[...]

    def step(k, unused):
        current = x_ref[...]
        lanes = lax.broadcasted_iota(jnp.int32, (1, size), 1)
        rows = lax.broadcasted_iota(jnp.int32, (size, 1), 0)
        row = x_ref[pl.ds(k, 1), :]
        pivot = jnp.sum(jnp.where(lanes == k, row, 0.0), axis=1, keepdims=True)
        column = jnp.sum(jnp.where(lanes == k, current, 0.0), axis=1, keepdims=True)
        column = jnp.where(rows == k, 0.0, column)
        scaled = jnp.where(lanes == k, 1.0, row) / pivot
        updated = jnp.where(lanes == k, 0.0, current) - column * scaled
        x_ref[...] = jnp.where(rows == k, scaled, updated)
        return unused

    lax.fori_loop(0, size, step, 0)


def invert(a_refs, x_refs):
    size = a_refs[0].shape[0]
    for a_ref, x_ref in zip(a_refs, x_refs):
        a = a_ref[...]
        norm = jnp.max(jnp.sum(jnp.abs(a), axis=0, keepdims=True))
        scale = 1.8 / norm
        x_ref[...] = jnp.where(eye_mask(size), 2.0 * scale, 0.0) - (scale * scale) * a

    def low_step(unused_step, unused):
        for a_ref, x_ref in zip(a_refs, x_refs):
            x = x_ref[...]
            xb = x.astype(BF16)
            r = jnp.where(eye_mask(size), 1.0, 0.0) - dot(a_ref[...].astype(BF16), xb)
            x_ref[...] = x + dot(xb, r.astype(BF16))
        return unused

    lax.fori_loop(0, LOW_STEPS, low_step, 0)

    def high_step(state):
        step, unused = state
        worst = jnp.zeros((1, 1), F32)
        for a_ref, x_ref in zip(a_refs, x_refs):
            x = x_ref[...]
            xs = split(x)
            r = jnp.where(eye_mask(size), 1.0, 0.0) - dot3(split(a_ref[...]), xs)
            square = jnp.sum(jnp.sum(r * r, axis=0, keepdims=True), axis=1, keepdims=True)
            worst = jnp.where(square <= worst, worst, square)
            x_ref[...] = x + dot(xs[0], r.astype(BF16))
        return step + 1, worst[0, 0]

    def again(state):
        step, worst = state
        return jnp.logical_and(step < HIGH_STEPS, jnp.logical_not(worst < CONVERGED**2))

    unused, worst = lax.while_loop(again, high_step, (jnp.int32(0), jnp.float32(1.0)))

    @pl.when(jnp.logical_not(worst < CONVERGED**2))
    def _():
        for a_ref, x_ref in zip(a_refs, x_refs):
            gauss_jordan(a_ref, x_ref)


def factor_kernel(
    faces, rates, library, walls, ph_ref, pl_ref, gh_ref, gl_ref, schur, inverse
):
    count = rates.shape[0]
    half = count // 2
    size = library.shape[1]

    def block(i):
        row = library[pl.ds(rates[i], 1), :]
        return jnp.where(eye_mask(size), row, 0.0) + walls[faces[i]] + walls[faces[i + 1]]

    def keep(i, side, coupling):
        x = inverse[side]
        xs = split(x)
        ph_ref[i], pl_ref[i] = xs
        q = split(coupling)
        gs = split(dot3(xs, q))
        gh_ref[i], gl_ref[i] = gs
        return dot3(q, gs)

    schur[0] = block(0)
    schur[1] = block(count - 1)

    def level(i, unused):
        j = count - 1 - i
        invert([schur.at[0], schur.at[1]], [inverse.at[0], inverse.at[1]])
        schur[0] = block(i + 1) - keep(i, 0, walls[faces[i + 1]])
        schur[1] = block(j - 1) - keep(j, 1, walls[faces[j]])
        return unused

    lax.fori_loop(0, half - 1, level, 0)
    invert([schur.at[1]], [inverse.at[1]])
    schur[0] = schur[0] - keep(half, 1, walls[faces[half]])
    invert([schur.at[0]], [inverse.at[0]])
    xs = split(inverse[0])
    ph_ref[half - 1], pl_ref[half - 1] = xs


def residual_kernel(index, side, near, library, out):
    for e in range(side.shape[0]):
        total = side[e]
        for d in range(4):
            total = total - dot3(split(near[e, d]), split(library[index[e, d]]), True)
        out[e] = total


def sweep_kernel(own, residual, ph_ref, pl_ref, gh_ref, gl_ref, out, values):
    count = residual.shape[0]
    half = count // 2

    def pivots(i):
        return ph_ref[i], pl_ref[i]

    def steps(i):
        return gh_ref[i], gl_ref[i]

    carried = [None] * count
    low, high = residual[0], residual[count - 1]
    for i in range(half):
        j = count - 1 - i
        carried[i], carried[j] = split(low), split(high)
        if i + 1 < half:
            low = residual[i + 1] + dot3(carried[i], steps(i))
            high = residual[j - 1] + dot3(carried[j], steps(j))
    scaled = {i: dot3(carried[i], pivots(i)) for i in range(count) if i != half - 1}
    low = dot3(split(low + dot3(carried[half], steps(half))), pivots(half - 1))
    values[half - 1] = low
    lows = split(low)
    high = scaled[half] + dot3(lows, steps(half), True)
    values[half] = high
    highs = split(high)
    for i in range(half - 2, -1, -1):
        j = count - 1 - i
        low = scaled[i] + dot3(lows, steps(i), True)
        high = scaled[j] + dot3(highs, steps(j), True)
        values[i] = low
        values[j] = high
        lows, highs = split(low), split(high)
    mine = out.shape[0]
    for e in range(mine):
        out[e] = values[own[0] * mine + e]


def on_device(
    right_side,
    old_values,
    element_library,
    wall_library,
    face_library,
    element_index,
    wall_faces,
    face_index,
):
    size = wall_library.shape[1]
    vmem = pl.BlockSpec(memory_space=pltpu.VMEM)
    smem = pl.BlockSpec(memory_space=pltpu.SMEM)
    params = pltpu.CompilerParams(vmem_limit_bytes=48 * 1024 * 1024)
    own = old_values[0, 0]
    near = []
    for axis in ("span", "stream"):
        n = lax.axis_size(axis)
        up = lax.ppermute(own, axis, [(i, (i + 1) % n) for i in range(n)])
        near.append(up)
        near.append(
            up if n == 2 else lax.ppermute(own, axis, [((i + 1) % n, i) for i in range(n)])
        )
    near = jnp.stack(near, axis=1)
    rows = jnp.concatenate([element_index[0, 0][:, None], wall_faces[0, 0]], axis=1)
    rows = lax.all_gather(rows, "wall", axis=0, tiled=True)
    rates = rows[:, 0]
    faces = jnp.concatenate([rows[:, 1], rows[-1:, 2]])
    count = rows.shape[0]
    blocks = jax.ShapeDtypeStruct((count, size, size), BF16)
    factors = pl.pallas_call(
        factor_kernel,
        out_shape=[blocks] * 4,
        in_specs=[smem, smem, vmem, vmem],
        out_specs=[vmem] * 4,
        scratch_shapes=[pltpu.VMEM((2, size, size), F32), pltpu.VMEM((2, size, size), F32)],
        compiler_params=params,
        cost_estimate=pl.CostEstimate(
            flops=400 * 2 * size**3, bytes_accessed=count * 8 * size * size, transcendentals=0
        ),
        name="factor_line",
    )(faces, rates, element_library, wall_library)
    residual = pl.pallas_call(
        residual_kernel,
        out_shape=jax.ShapeDtypeStruct(own.shape, F32),
        in_specs=[smem, vmem, vmem, vmem],
        out_specs=vmem,
        compiler_params=params,
        name="residual",
    )(face_index[0, 0], right_side[0, 0], near, face_library)
    residual = lax.all_gather(residual, "wall", axis=0, tiled=True)
    place = jnp.reshape(lax.axis_index("wall"), (1,)).astype(jnp.int32)
    new_values = pl.pallas_call(
        sweep_kernel,
        out_shape=jax.ShapeDtypeStruct(own.shape, F32),
        in_specs=[smem] + [vmem] * 5,
        out_specs=vmem,
        scratch_shapes=[pltpu.VMEM((count,) + own.shape[1:], F32)],
        compiler_params=params,
        name="sweep",
    )(place, residual, *factors)
    return new_values[None, None]


def solution(mesh):
    placed = (
        P("span", "stream", "wall", None, None),
        P("span", "stream", "wall", None, None),
        P(),
        P(),
        P(),
        P("span", "stream", "wall"),
        P("span", "stream", "wall", None),
        P("span", "stream", "wall", None),
    )
    return jax.shard_map(
        on_device,
        mesh=mesh,
        in_specs=placed,
        out_specs=P("span", "stream", "wall", None, None),
        check_vma=False,
    )
```

```python
import functools
import jax
import jax.numpy as jnp
from jax import lax
from jax.experimental import pallas as pl
from jax.experimental.pallas import tpu as pltpu
from jax.sharding import PartitionSpec as P

F32 = jnp.float32
BF16 = jnp.bfloat16
LOW_STEPS = 2
HIGH_STEPS = 4
CONVERGED = 0.08


def dot(a, b, transposed=False):
    dims = (((1,), (1,)), ((), ())) if transposed else (((1,), (0,)), ((), ()))
    return lax.dot_general(a, b, dims, preferred_element_type=F32)


def split(a):
    high = a.astype(BF16)
    return high, (a - high.astype(F32)).astype(BF16)


def dot3(a, b, transposed=False):
    return (
        dot(a[0], b[0], transposed) + (dot(a[0], b[1], transposed) + dot(a[1], b[0], transposed))
    )


def eye_mask(size):
    row = lax.broadcasted_iota(jnp.int32, (size, size), 0)
    col = lax.broadcasted_iota(jnp.int32, (size, size), 1)
    return row == col


def gauss_jordan(a_ref, x_ref):
    size = a_ref.shape[0]
    x_ref[...] = a_ref[...]

    def step(k, unused):
        current = x_ref[...]
        lanes = lax.broadcasted_iota(jnp.int32, (1, size), 1)
        rows = lax.broadcasted_iota(jnp.int32, (size, 1), 0)
        row = x_ref[pl.ds(k, 1), :]
        pivot = jnp.sum(jnp.where(lanes == k, row, 0.0), axis=1, keepdims=True)
        column = jnp.sum(jnp.where(lanes == k, current, 0.0), axis=1, keepdims=True)
        column = jnp.where(rows == k, 0.0, column)
        scaled = jnp.where(lanes == k, 1.0, row) / pivot
        updated = jnp.where(lanes == k, 0.0, current) - column * scaled
        x_ref[...] = jnp.where(rows == k, scaled, updated)
        return unused

    lax.fori_loop(0, size, step, 0)


def refine(a_ref, x_ref):
    x = x_ref[...]
    xs = split(x)
    r = jnp.where(eye_mask(x.shape[0]), 1.0, 0.0) - dot3(split(a_ref[...]), xs)
    rb = r.astype(BF16)
    x_ref[...] = x + dot(xs[0], (r + dot(rb, rb)).astype(BF16))
    return jnp.sum(jnp.sum(r * r, axis=0, keepdims=True), axis=1, keepdims=True)


def invert(a_refs, x_refs):
    size = a_refs[0].shape[0]
    pairs = list(zip(a_refs, x_refs))
    mask = eye_mask(size)
    lows, xs = [], []
    for a_ref, unused in pairs:
        a = a_ref[...]
        trace = jnp.sum(jnp.sum(jnp.where(mask, a, 0.0), axis=0, keepdims=True), axis=1, keepdims=True)
        square = jnp.sum(jnp.sum(a * a, axis=0, keepdims=True), axis=1, keepdims=True)
        scale = trace / square
        xs.append(jnp.where(mask, 2.0 * scale, 0.0) - (scale * scale) * a)
        lows.append(a.astype(BF16))
    for step in range(LOW_STEPS):
        xbs = [x.astype(BF16) for x in xs]
        rs = [jnp.where(mask, 1.0, 0.0) - dot(low, xb) for low, xb in zip(lows, xbs)]
        xs = [x + dot(xb, r.astype(BF16)) for x, xb, r in zip(xs, xbs, rs)]
    for (unused, x_ref), x in zip(pairs, xs):
        x_ref[...] = x
    worst = sum(refine(a_ref, x_ref) for a_ref, x_ref in pairs)[0, 0]

    @pl.when(jnp.logical_not(worst < CONVERGED**2))
    def _():
        def again(state):
            step, now = state
            return jnp.logical_and(step < HIGH_STEPS, jnp.logical_not(now < CONVERGED**2))

        def more(state):
            return state[0] + 1, sum(refine(*pair) for pair in pairs)[0, 0]

        unused, last = lax.while_loop(again, more, (jnp.int32(0), worst))

        @pl.when(jnp.logical_not(last < CONVERGED**2))
        def _():
            for pair in pairs:
                gauss_jordan(*pair)


class Line:
    def __init__(self, rows, library, walls, table):
        self.library, self.walls, self.table = library, walls, table
        count = len(rows)
        mine = rows[0].shape[0]
        place = lax.axis_index("wall")
        for shift, ref in enumerate(rows):
            owner = lax.rem(place - shift + count, count)
            for e in range(mine):
                for c in range(3):
                    table[owner * mine + e, c] = ref[e, c]
        self.count = count * mine
        self.size = walls.shape[1]

    def face(self, i):
        if i == self.count:
            return self.walls[self.table[i - 1, 2]]
        return self.walls[self.table[i, 1]]

    def block(self, i):
        row = self.library[pl.ds(self.table[i, 0], 1), :]
        return jnp.where(eye_mask(self.size), row, 0.0) + self.face(i) + self.face(i + 1)


def keep(x_ref, coupling, stores, slot):
    xs = split(x_ref[...])
    q = split(coupling)
    gs = split(dot3(xs, q))
    for store, value in zip(stores, xs + gs):
        store[slot] = value
    return dot3(q, gs)


def levels_kernel(first, last, wall_count, with_middle, *refs):
    rows, (library, walls) = refs[:wall_count], refs[wall_count : wall_count + 2]
    refs = refs[wall_count + 2 :]
    before = refs[0] if first > 0 else None
    refs = refs[1:] if first > 0 else refs
    schur, stores, (inverse, table) = refs[0], refs[1:5], refs[5:]
    line = Line(rows, library, walls, table)
    top = line.count - 1
    if first > 0:
        schur[...] = before[...]
    else:
        schur[0] = line.block(0)
        schur[1] = line.block(top)
    for i in range(first, last):
        slot = 2 * (i - first)
        invert([schur.at[0], schur.at[1]], [inverse.at[0], inverse.at[1]])
        low = keep(inverse.at[0], line.face(i + 1), stores, slot)
        high = keep(inverse.at[1], line.face(top - i), stores, slot + 1)
        schur[0] = line.block(i + 1) - low
        schur[1] = line.block(top - i - 1) - high
    if with_middle:
        invert([schur.at[1]], [inverse.at[1]])
        schur[0] = schur[0] - keep(
            inverse.at[1], line.face(line.count // 2), stores, 2 * (last - first)
        )


def residual_kernel(index, side, near_0, near_1, near_2, near_3, library, out):
    near = (near_0, near_1, near_2, near_3)
    for e in range(side.shape[0]):
        total = side[e]
        for d in range(4):
            total = total - dot3(split(near[d][e]), split(library[index[e, d]]), True)
        out[e] = total


def sweep_kernel(wall_count, split_level, *refs):
    sides, refs = refs[:wall_count], refs[wall_count:]
    schur, early, late, (out, residual, values, inverse) = refs[0], refs[1:5], refs[5:9], refs[9:]
    mine = out.shape[0]
    place = lax.axis_index("wall")
    for shift, ref in enumerate(sides):
        owner = lax.rem(place - shift + wall_count, wall_count)
        for e in range(mine):
            residual[owner * mine + e] = ref[e]
    count = wall_count * mine
    half = count // 2

    def part(i, which):
        level = i if i < half else count - 1 - i
        side = 0 if i < half else 1
        store, base = (early, 0) if level < split_level else (late, split_level)
        slot = 2 * (level - base) + (side if level < half - 1 else 0)
        return store[2 * which][slot], store[2 * which + 1][slot]

    invert([schur.at[0]], [inverse])
    carried = [None] * count
    low, high = residual[0], residual[count - 1]
    for i in range(half):
        j = count - 1 - i
        carried[i], carried[j] = split(low), split(high)
        if i + 1 < half:
            low = residual[i + 1] + dot3(carried[i], part(i, 1))
            high = residual[j - 1] + dot3(carried[j], part(j, 1))
    scaled = {i: dot3(carried[i], part(i, 0)) for i in range(count) if i != half - 1}
    low = low + dot3(carried[half], part(half, 1))
    low = dot3(split(low), split(inverse[...]))
    values[half - 1] = low
    lows = split(low)
    high = scaled[half] + dot3(lows, part(half, 1), True)
    values[half] = high
    highs = split(high)
    for i in range(half - 2, -1, -1):
        j = count - 1 - i
        low = scaled[i] + dot3(lows, part(i, 1), True)
        high = scaled[j] + dot3(highs, part(j, 1), True)
        values[i] = low
        values[j] = high
        lows, highs = split(low), split(high)
    for e in range(mine):
        out[e] = values[place * mine + e]


def on_device(
    right_side,
    old_values,
    element_library,
    wall_library,
    face_library,
    element_index,
    wall_faces,
    face_index,
):
    size = wall_library.shape[1]
    vmem = pl.BlockSpec(memory_space=pltpu.VMEM)
    smem = pl.BlockSpec(memory_space=pltpu.SMEM)
    params = pltpu.CompilerParams(vmem_limit_bytes=28 * 1024 * 1024)
    wall_count = lax.axis_size("wall")
    own = old_values[0, 0]
    mine = own.shape[0]
    count = wall_count * mine
    half = count // 2

    def shifted(array, axis, shift):
        n = lax.axis_size(axis)
        return lax.ppermute(array, axis, [(i, (i + shift) % n) for i in range(n)])

    rows = jnp.concatenate([element_index[0, 0][:, None], wall_faces[0, 0]], axis=1)
    rows = [rows] + [shifted(rows, "wall", s) for s in range(1, wall_count)]
    near = []
    for axis in ("span", "stream"):
        up = shifted(own, axis, 1)
        near += [up, up if lax.axis_size(axis) == 2 else shifted(own, axis, -1)]

    def factor(first, last, with_middle, schur, name):
        slots = 2 * (last - first) + int(with_middle)
        blocks = jax.ShapeDtypeStruct((slots, size, size), BF16)
        return pl.pallas_call(
            functools.partial(levels_kernel, first, last, wall_count, with_middle),
            out_shape=[jax.ShapeDtypeStruct((2, size, size), F32)] + [blocks] * 4,
            in_specs=[smem] * wall_count + [vmem] * (2 + len(schur)),
            out_specs=[vmem] * 5,
            scratch_shapes=[pltpu.VMEM((2, size, size), F32), pltpu.SMEM((count, 3), jnp.int32)],
            compiler_params=params,
            cost_estimate=pl.CostEstimate(
                flops=slots * 160 * size**3, bytes_accessed=16 * size * size, transcendentals=0
            ),
            name=name,
        )(*rows, element_library, wall_library, *schur)

    cut = max(1, half - 2)
    schur, *early = factor(0, cut, False, [], "factor_outer")
    schur, *near = lax.optimization_barrier((schur, *near))
    residual = pl.pallas_call(
        residual_kernel,
        out_shape=jax.ShapeDtypeStruct(own.shape, F32),
        in_specs=[smem] + [vmem] * 6,
        out_specs=vmem,
        compiler_params=params,
        name="residual",
    )(face_index[0, 0], right_side[0, 0], *near, face_library)
    schur, residual = lax.optimization_barrier((schur, residual))
    sides = [residual] + [shifted(residual, "wall", s) for s in range(1, wall_count)]
    schur, *late = factor(cut, half - 1, True, [schur], "factor_inner")
    new_values = pl.pallas_call(
        functools.partial(sweep_kernel, wall_count, cut),
        out_shape=jax.ShapeDtypeStruct(own.shape, F32),
        in_specs=[vmem] * (wall_count + 9),
        out_specs=vmem,
        scratch_shapes=[
            pltpu.VMEM((count,) + own.shape[1:], F32),
            pltpu.VMEM((count,) + own.shape[1:], F32),
            pltpu.VMEM((size, size), F32),
        ],
        compiler_params=params,
        name="sweep",
    )(*sides, schur, *early, *late)
    return new_values[None, None]


def solution(mesh):
    placed = (
        P("span", "stream", "wall", None, None),
        P("span", "stream", "wall", None, None),
        P(),
        P(),
        P(),
        P("span", "stream", "wall"),
        P("span", "stream", "wall", None),
        P("span", "stream", "wall", None),
    )
    return jax.shard_map(
        on_device,
        mesh=mesh,
        in_specs=placed,
        out_specs=P("span", "stream", "wall", None, None),
        check_vma=False,
    )
```

```python
import functools
import jax
import jax.numpy as jnp
from jax import lax
from jax.experimental import pallas as pl
from jax.experimental.pallas import tpu as pltpu
from jax.sharding import PartitionSpec as P

F32 = jnp.float32
BF16 = jnp.bfloat16
LOW_STEPS = 2
HIGH_STEPS = 12
CONVERGED = 0.08


def dot(a, b, transposed=False):
    dims = (((1,), (1,)), ((), ())) if transposed else (((1,), (0,)), ((), ()))
    return lax.dot_general(a, b, dims, preferred_element_type=F32)


def split(a):
    high = a.astype(BF16)
    return high, (a - high.astype(F32)).astype(BF16)


def dot3(a, b, transposed=False):
    if transposed:
        return dot(a[0], b[0], True) + (dot(a[0], b[1], True) + dot(a[1], b[0], True))
    left = jnp.concatenate([a[0], a[0], a[1]], axis=1)
    return dot(left, jnp.concatenate([b[0], b[1], b[0]], axis=0))


def eye_mask(size):
    row = lax.broadcasted_iota(jnp.int32, (size, size), 0)
    col = lax.broadcasted_iota(jnp.int32, (size, size), 1)
    return row == col


def gauss_jordan(a_ref, x_ref):
    size = a_ref.shape[0]
    x_ref[...] = a_ref[...]

    def step(k, unused):
        current = x_ref[...]
        lanes = lax.broadcasted_iota(jnp.int32, (1, size), 1)
        rows = lax.broadcasted_iota(jnp.int32, (size, 1), 0)
        row = x_ref[pl.ds(k, 1), :]
        pivot = jnp.sum(jnp.where(lanes == k, row, 0.0), axis=1, keepdims=True)
        column = jnp.sum(jnp.where(lanes == k, current, 0.0), axis=1, keepdims=True)
        column = jnp.where(rows == k, 0.0, column)
        scaled = jnp.where(lanes == k, 1.0, row) / pivot
        updated = jnp.where(lanes == k, 0.0, current) - column * scaled
        x_ref[...] = jnp.where(rows == k, scaled, updated)
        return unused

    lax.fori_loop(0, size, step, 0)


def refine(a_ref, x_ref):
    x = x_ref[...]
    xs = split(x)
    r = jnp.where(eye_mask(x.shape[0]), 1.0, 0.0) - dot3(split(a_ref[...]), xs)
    rb = r.astype(BF16)
    x_ref[...] = x + dot(xs[0], (r + dot(rb, rb)).astype(BF16))
    return jnp.sum(jnp.sum(r * r, axis=0, keepdims=True), axis=1, keepdims=True)


def invert(a_refs, x_refs, low_steps=LOW_STEPS):
    size = a_refs[0].shape[0]
    pairs = list(zip(a_refs, x_refs))
    mask = eye_mask(size)
    lows, xs = [], []
    for a_ref, unused in pairs:
        a = a_ref[...]
        diagonal = jnp.where(mask, a, 0.0)
        row = 1.0 / jnp.sum(diagonal, axis=0, keepdims=True)
        col = 1.0 / jnp.sum(diagonal, axis=1, keepdims=True)
        scaled = a * row * col
        square = jnp.sum(jnp.sum(a * scaled, axis=0, keepdims=True), axis=1, keepdims=True)
        scale = size / square
        xs.append(jnp.where(mask, 2.0 * scale * row, 0.0) - (scale * scale) * scaled)
        lows.append(a.astype(BF16))
    for step in range(low_steps):
        xbs = [x.astype(BF16) for x in xs]
        rs = [jnp.where(mask, 1.0, 0.0) - dot(low, xb) for low, xb in zip(lows, xbs)]
        xs = [x + dot(xb, r.astype(BF16)) for x, xb, r in zip(xs, xbs, rs)]
    for (unused, x_ref), x in zip(pairs, xs):
        x_ref[...] = x
    worst = sum(refine(a_ref, x_ref) for a_ref, x_ref in pairs)[0, 0]

    @pl.when(jnp.logical_not(worst < CONVERGED**2))
    def _():
        @pl.when(jnp.logical_not(worst < 0.25))
        def _():
            for a_ref, x_ref in pairs:
                a = a_ref[...]
                row = 1.0 / jnp.sum(jnp.where(mask, a, 0.0), axis=0, keepdims=True)
                norm = jnp.max(jnp.sum(jnp.abs(a) * row, axis=1, keepdims=True), axis=0, keepdims=True)
                x_ref[...] = jnp.where(mask, row / norm, 0.0)

        def again(state):
            step, now = state
            return jnp.logical_and(step < HIGH_STEPS, jnp.logical_not(now < CONVERGED**2))

        def more(state):
            return state[0] + 1, sum(refine(*pair) for pair in pairs)[0, 0]

        unused, last = lax.while_loop(again, more, (jnp.int32(0), worst))

        @pl.when(jnp.logical_not(last < CONVERGED**2))
        def _():
            for pair in pairs:
                gauss_jordan(*pair)


class Line:
    def __init__(self, rows, library, walls, table):
        self.library, self.walls, self.table = library, walls, table
        count = len(rows)
        mine = rows[0].shape[0]
        place = lax.axis_index("wall")
        for shift, ref in enumerate(rows):
            owner = lax.rem(place - shift + count, count)
            for e in range(mine):
                for c in range(3):
                    table[owner * mine + e, c] = ref[e, c]
        self.count = count * mine
        self.size = walls.shape[1]

    def face(self, i):
        if i == self.count:
            return self.walls[self.table[i - 1, 2]]
        return self.walls[self.table[i, 1]]

    def block(self, i):
        row = self.library[pl.ds(self.table[i, 0], 1), :]
        return jnp.where(eye_mask(self.size), row, 0.0) + self.face(i) + self.face(i + 1)


def keep(x_ref, coupling, stores, slot):
    xs = split(x_ref[...])
    q = split(coupling)
    gs = split(dot3(xs, q))
    for store, value in zip(stores, xs + gs):
        store[slot] = value
    return dot3(q, gs)


def levels_kernel(first, last, wall_count, with_middle, *refs):
    rows, (library, walls) = refs[:wall_count], refs[wall_count : wall_count + 2]
    refs = refs[wall_count + 2 :]
    before = refs[0] if first > 0 else None
    refs = refs[1:] if first > 0 else refs
    schur, stores, (inverse, table) = refs[0], refs[1:5], refs[5:]
    line = Line(rows, library, walls, table)
    top = line.count - 1
    if first > 0:
        schur[...] = before[...]
    else:
        schur[0] = line.block(0)
        schur[1] = line.block(top)
    for i in range(first, last):
        slot = 2 * (i - first)
        invert([schur.at[0], schur.at[1]], [inverse.at[0], inverse.at[1]])
        low = keep(inverse.at[0], line.face(i + 1), stores, slot)
        high = keep(inverse.at[1], line.face(top - i), stores, slot + 1)
        schur[0] = line.block(i + 1) - low
        schur[1] = line.block(top - i - 1) - high
    if with_middle:
        invert([schur.at[1]], [inverse.at[1]])
        schur[0] = schur[0] - keep(
            inverse.at[1], line.face(line.count // 2), stores, 2 * (last - first)
        )


def residual_kernel(index, side, near_0, near_1, near_2, near_3, library, out):
    near = (near_0, near_1, near_2, near_3)
    for e in range(side.shape[0]):
        total = side[e]
        for d in range(4):
            total = total - dot3(split(near[d][e]), split(library[index[e, d]]), True)
        out[e] = total


def sweep_kernel(wall_count, split_level, *refs):
    sides, refs = refs[:wall_count], refs[wall_count:]
    schur, early, late, (out, residual, values, inverse) = refs[0], refs[1:5], refs[5:9], refs[9:]
    mine = out.shape[0]
    place = lax.axis_index("wall")
    for shift, ref in enumerate(sides):
        owner = lax.rem(place - shift + wall_count, wall_count)
        for e in range(mine):
            residual[owner * mine + e] = ref[e]
    count = wall_count * mine
    half = count // 2

    def part(i, which):
        level = i if i < half else count - 1 - i
        side = 0 if i < half else 1
        store, base = (early, 0) if level < split_level else (late, split_level)
        slot = 2 * (level - base) + (side if level < half - 1 else 0)
        return store[2 * which][slot], store[2 * which + 1][slot]

    invert([schur.at[0]], [inverse], 1)
    carried = [None] * count
    low, high = residual[0], residual[count - 1]
    for i in range(half):
        j = count - 1 - i
        carried[i], carried[j] = split(low), split(high)
        if i + 1 < half:
            low = residual[i + 1] + dot3(carried[i], part(i, 1))
            high = residual[j - 1] + dot3(carried[j], part(j, 1))
    scaled = {i: dot3(carried[i], part(i, 0)) for i in range(count) if i != half - 1}
    low = low + dot3(carried[half], part(half, 1))
    low = dot3(split(low), split(inverse[...]))
    values[half - 1] = low
    lows = split(low)
    high = scaled[half] + dot3(lows, part(half, 1), True)
    values[half] = high
    highs = split(high)
    for i in range(half - 2, -1, -1):
        j = count - 1 - i
        low = scaled[i] + dot3(lows, part(i, 1), True)
        high = scaled[j] + dot3(highs, part(j, 1), True)
        values[i] = low
        values[j] = high
        lows, highs = split(low), split(high)
    for e in range(mine):
        out[e] = values[place * mine + e]


def on_device(
    right_side,
    old_values,
    element_library,
    wall_library,
    face_library,
    element_index,
    wall_faces,
    face_index,
):
    size = wall_library.shape[1]
    vmem = pl.BlockSpec(memory_space=pltpu.VMEM)
    smem = pl.BlockSpec(memory_space=pltpu.SMEM)
    params = pltpu.CompilerParams(vmem_limit_bytes=28 * 1024 * 1024)
    wall_count = lax.axis_size("wall")
    own = old_values[0, 0]
    mine = own.shape[0]
    count = wall_count * mine
    half = count // 2

    def shifted(array, axis, shift):
        n = lax.axis_size(axis)
        return lax.ppermute(array, axis, [(i, (i + shift) % n) for i in range(n)])

    rows = jnp.concatenate([element_index[0, 0][:, None], wall_faces[0, 0]], axis=1)
    rows = [rows] + [shifted(rows, "wall", s) for s in range(1, wall_count)]
    near = []
    for axis in ("span", "stream"):
        up = shifted(own, axis, 1)
        near += [up, up if lax.axis_size(axis) == 2 else shifted(own, axis, -1)]

    def factor(first, last, with_middle, schur, name):
        slots = 2 * (last - first) + int(with_middle)
        blocks = jax.ShapeDtypeStruct((slots, size, size), BF16)
        return pl.pallas_call(
            functools.partial(levels_kernel, first, last, wall_count, with_middle),
            out_shape=[jax.ShapeDtypeStruct((2, size, size), F32)] + [blocks] * 4,
            in_specs=[smem] * wall_count + [vmem] * (2 + len(schur)),
            out_specs=[vmem] * 5,
            scratch_shapes=[pltpu.VMEM((2, size, size), F32), pltpu.SMEM((count, 3), jnp.int32)],
            compiler_params=params,
            cost_estimate=pl.CostEstimate(
                flops=slots * 160 * size**3, bytes_accessed=16 * size * size, transcendentals=0
            ),
            name=name,
        )(*rows, element_library, wall_library, *schur)

    cut = max(1, half - 2)
    schur, *early = factor(0, cut, False, [], "factor_outer")
    schur, *near = lax.optimization_barrier((schur, *near))
    residual = pl.pallas_call(
        residual_kernel,
        out_shape=jax.ShapeDtypeStruct(own.shape, F32),
        in_specs=[smem] + [vmem] * 6,
        out_specs=vmem,
        compiler_params=params,
        name="residual",
    )(face_index[0, 0], right_side[0, 0], *near, face_library)
    schur, residual = lax.optimization_barrier((schur, residual))
    sides = [residual] + [shifted(residual, "wall", s) for s in range(1, wall_count)]
    schur, *late = factor(cut, half - 1, True, [schur], "factor_inner")
    new_values = pl.pallas_call(
        functools.partial(sweep_kernel, wall_count, cut),
        out_shape=jax.ShapeDtypeStruct(own.shape, F32),
        in_specs=[vmem] * (wall_count + 9),
        out_specs=vmem,
        scratch_shapes=[
            pltpu.VMEM((count,) + own.shape[1:], F32),
            pltpu.VMEM((count,) + own.shape[1:], F32),
            pltpu.VMEM((size, size), F32),
        ],
        compiler_params=params,
        name="sweep",
    )(*sides, schur, *early, *late)
    return new_values[None, None]


def solution(mesh):
    placed = (
        P("span", "stream", "wall", None, None),
        P("span", "stream", "wall", None, None),
        P(),
        P(),
        P(),
        P("span", "stream", "wall"),
        P("span", "stream", "wall", None),
        P("span", "stream", "wall", None),
    )
    return jax.shard_map(
        on_device,
        mesh=mesh,
        in_specs=placed,
        out_specs=P("span", "stream", "wall", None, None),
        check_vma=False,
    )
```

```python
import functools
import jax
import jax.numpy as jnp
from jax import lax
from jax.experimental import pallas as pl
from jax.experimental.pallas import tpu as pltpu
from jax.sharding import PartitionSpec as P

F32 = jnp.float32
BF16 = jnp.bfloat16
LOW_STEPS = 2
CONVERGED = 0.08
MESH = pl.DeviceIdType.MESH


def dot(a, b, transposed=False):
    dims = (((1,), (1,)), ((), ())) if transposed else (((1,), (0,)), ((), ()))
    return lax.dot_general(a, b, dims, preferred_element_type=F32)


def split(a):
    high = a.astype(BF16)
    return high, (a - high.astype(F32)).astype(BF16)


def dot3(a, b, transposed=False):
    if transposed:
        return dot(a[0], b[0], True) + (dot(a[0], b[1], True) + dot(a[1], b[0], True))
    left = jnp.concatenate([a[0], a[0], a[1]], axis=1)
    return dot(left, jnp.concatenate([b[0], b[1], b[0]], axis=0))


def eye_mask(size):
    row = lax.broadcasted_iota(jnp.int32, (size, size), 0)
    col = lax.broadcasted_iota(jnp.int32, (size, size), 1)
    return row == col


def gauss_jordan(a_ref, x_ref):
    size = a_ref.shape[0]
    x_ref[...] = a_ref[...]

    def step(k, unused):
        current = x_ref[...]
        lanes = lax.broadcasted_iota(jnp.int32, (1, size), 1)
        rows = lax.broadcasted_iota(jnp.int32, (size, 1), 0)
        row = x_ref[pl.ds(k, 1), :]
        pivot = jnp.sum(jnp.where(lanes == k, row, 0.0), axis=1, keepdims=True)
        column = jnp.sum(jnp.where(lanes == k, current, 0.0), axis=1, keepdims=True)
        column = jnp.where(rows == k, 0.0, column)
        scaled = jnp.where(lanes == k, 1.0, row) / pivot
        updated = jnp.where(lanes == k, 0.0, current) - column * scaled
        x_ref[...] = jnp.where(rows == k, scaled, updated)
        return unused

    lax.fori_loop(0, size, step, 0)


def invert(blocks, low_steps=LOW_STEPS):
    size = blocks[0].shape[0]
    mask = eye_mask(size)
    xs = []
    for a in blocks:
        diagonal = jnp.where(mask, a, 0.0)
        row = 1.0 / jnp.sum(diagonal, axis=0, keepdims=True)
        col = 1.0 / jnp.sum(diagonal, axis=1, keepdims=True)
        scaled = a * row * col
        square = jnp.sum(jnp.sum(a * scaled, axis=0, keepdims=True), axis=1, keepdims=True)
        scale = size / square
        xs.append(jnp.where(mask, 2.0 * scale * row, 0.0) - (scale * scale) * scaled)
    parts = [split(a) for a in blocks]
    for step in range(low_steps):
        xbs = [x.astype(BF16) for x in xs]
        rs = [jnp.where(mask, 1.0, 0.0) - dot(a[0], xb) for a, xb in zip(parts, xbs)]
        xs = [x + dot(xb, r.astype(BF16)) for x, xb, r in zip(xs, xbs, rs)]
    halves = [split(x) for x in xs]
    rs = [jnp.where(mask, 1.0, 0.0) - dot3(a, x) for a, x in zip(parts, halves)]
    rbs = [r.astype(BF16) for r in rs]
    ts = [r + dot(rb, rb) for r, rb in zip(rs, rbs)]
    xs = [x + dot(h[0], t.astype(BF16)) for x, h, t in zip(xs, halves, ts)]
    missed = jnp.zeros((1, 1), F32)
    for r in rs:
        square = jnp.sum(jnp.sum(r * r, axis=0, keepdims=True), axis=1, keepdims=True)
        missed = missed + jnp.where(square < CONVERGED**2, 0.0, 1.0)
    return xs, missed


class Line:
    def __init__(self, index, mine, library, walls):
        self.library, self.walls = library, walls
        self.rates, self.faces = [], []
        for owner in range(index.shape[0]):
            rows = index[owner]
            for e in range(mine):
                self.rates.append(rows[e, 0])
                self.faces.append(rows[e, 1])
        self.faces.append(rows[mine - 1, 2])
        self.count = len(self.rates)
        self.size = walls.shape[1]

    def face(self, i):
        return self.walls[self.faces[i]]

    def block(self, i):
        row = self.library[pl.ds(self.rates[i], 1), :]
        return jnp.where(eye_mask(self.size), row, 0.0) + self.face(i) + self.face(i + 1)


def keep(i, x, coupling, stores):
    xs = split(x)
    q = split(coupling)
    gs = split(dot3(xs, q))
    for store, value in zip(stores, xs + gs):
        store[i] = value
    return dot3(q, gs)


class Sweep:
    def __init__(self, count, stores, residual):
        self.count, self.half, self.stores, self.residual = count, count // 2, stores, residual

    def pivot(self, i):
        return self.stores[0][i], self.stores[1][i]

    def step(self, i):
        return self.stores[2][i], self.stores[3][i]

    def forward(self):
        count, half, residual = self.count, self.half, self.residual
        carried = [None] * count
        low, high = residual(0), residual(count - 1)
        for i in range(half):
            j = count - 1 - i
            carried[i], carried[j] = split(low), split(high)
            if i + 1 < half:
                low = residual(i + 1) + dot3(carried[i], self.step(i))
                high = residual(j - 1) + dot3(carried[j], self.step(j))
        skip = (half - 1, half)
        self.scaled = {
            i: dot3(carried[i], self.pivot(i)) for i in range(count) if i not in skip
        }
        self.low, self.carried = low, carried[half]

    def back(self, inverse, values):
        count, half = self.count, self.half
        low = self.low + dot3(self.carried, self.step(half))
        middle = dot3(self.carried, self.pivot(half))
        low = dot3(split(low), split(inverse))
        values[half - 1] = low
        lows = split(low)
        high = middle + dot3(lows, self.step(half), True)
        values[half] = high
        highs = split(high)
        for i in range(half - 2, -1, -1):
            j = count - 1 - i
            low = self.scaled[i] + dot3(lows, self.step(i), True)
            high = self.scaled[j] + dot3(highs, self.step(j), True)
            values[i] = low
            values[j] = high
            lows, highs = split(low), split(high)


def line_kernel(
    rates, faces, neighbours, side_in, old, library_in, walls_in, blocks_in,
    out, sides_out, index_out, missed_out,
    side, library, walls, blocks, index, halo, sides, values, ph, plo, gh, glo,
    local_sem, index_send, index_recv, halo_send, halo_recv, side_send, side_recv,
):
    n = lax.axis_size("wall")
    place = lax.axis_index("wall")
    mine = side.shape[0]
    count = n * mine
    half = count // 2
    top = count - 1

    pairs = ((walls_in, walls), (library_in, library), (side_in.at[0, 0], side), (blocks_in, blocks))
    loads = [
        pltpu.make_async_copy(src, dst, local_sem.at[k]) for k, (src, dst) in enumerate(pairs)
    ]
    for load in loads:
        load.start()

    row = lax.broadcasted_iota(jnp.int32, index.shape[1:], 0)
    col = lax.broadcasted_iota(jnp.int32, index.shape[1:], 1)
    own = jnp.zeros(index.shape[1:], jnp.int32)
    for e in range(mine):
        for c, value in enumerate((rates[0, 0, e], faces[0, 0, e, 0], faces[0, 0, e, 1])):
            own = jnp.where(jnp.logical_and(row == e, col == c), value, own)
    index[place] = own

    partners = [{"wall": lax.rem(place + s, n)} for s in range(1, n)]
    beside = []
    for base, axis in ((0, "span"), (2, "stream")):
        m = lax.axis_size(axis)
        here = lax.axis_index(axis)
        beside.append((base, {axis: lax.rem(here + 1, m)}))
        if m > 2:
            beside.append((base + 1, {axis: lax.rem(here + m - 1, m)}))
    barrier = pltpu.get_barrier_semaphore()
    for target in partners + [target for unused, target in beside]:
        pl.semaphore_signal(barrier, inc=1, device_id=target, device_id_type=MESH)
    pl.semaphore_wait(barrier, len(partners) + len(beside))

    def spread(buffer, send, recv):
        copies = [
            pltpu.make_async_remote_copy(
                src_ref=buffer.at[place],
                dst_ref=buffer.at[place],
                send_sem=send.at[k],
                recv_sem=recv.at[k],
                device_id=target,
                device_id_type=MESH,
            )
            for k, target in enumerate(partners)
        ]
        for copy in copies:
            copy.start()
        return copies

    index_copies = spread(index, index_send, index_recv)
    halo_copies = [
        pltpu.make_async_remote_copy(
            src_ref=old.at[0, 0],
            dst_ref=halo.at[k],
            send_sem=halo_send.at[k],
            recv_sem=halo_recv.at[k],
            device_id=target,
            device_id_type=MESH,
        )
        for k, target in beside
    ]
    for copy in halo_copies:
        copy.start()
    for load in loads[:2]:
        load.wait()
    for copy in index_copies:
        copy.wait()
    line = Line(index, mine, library, walls)
    stores = (ph, plo, gh, glo)
    low, high = line.block(0), line.block(top)
    missed = jnp.zeros((1, 1), F32)
    side_copies = None
    for i in range(half - 1):
        j = top - i
        (x, y), off = invert([low, high])
        missed = missed + off
        low = line.block(i + 1) - keep(i, x, line.face(i + 1), stores)
        high = line.block(j - 1) - keep(j, y, line.face(j), stores)
        if i == max(0, half - 3):
            for load in loads[2:]:
                load.wait()
            for copy in halo_copies:
                copy.wait()
            arrived = [k for k, unused in beside]
            for e in range(mine):
                total = side[e]
                for d in range(4):
                    near = halo[d if d in arrived else d - 1, e]
                    block = blocks[neighbours[0, 0, e, d]]
                    total = total - dot3(split(near), split(block), True)
                sides[place, e] = total
            side_copies = spread(sides, side_send, side_recv)
    for copy in side_copies:
        copy.wait()
    sweep = Sweep(count, stores, lambda i: sides[i // mine, i % mine])
    sweep.forward()
    (y,), off = invert([high])
    missed = missed + off
    low = low - keep(half, y, line.face(half), stores)
    (x,), off = invert([low], 1)
    missed = missed + off
    sweep.back(x, values)
    for e in range(mine):
        out[0, 0, e] = values[place * mine + e]
    sides_out[...] = sides[...]
    index_out[...] = index[...]
    missed_out[...] = jnp.broadcast_to(missed, missed_out.shape)


def check_kernel(
    missed, fast, sides_in, index_in, library_in, walls_in,
    out, sides, index, library, walls, values, block, inverse, ph, plo, gh, glo,
):
    out[...] = fast[...]

    @pl.when(jnp.logical_not(missed[0:1, 0:1][0, 0] < 0.5))
    def _():
        for src, dst in (
            (sides_in, sides), (index_in, index), (library_in, library), (walls_in, walls)
        ):
            pltpu.sync_copy(src, dst)
        n, mine = sides.shape[:2]
        count = n * mine
        half = count // 2
        place = lax.axis_index("wall")
        line = Line(index, mine, library, walls)
        stores = (ph, plo, gh, glo)

        def exact(a):
            block[...] = a
            gauss_jordan(block, inverse)
            return inverse[...]

        low = line.block(0)
        high = line.block(count - 1)
        for i in range(half - 1):
            j = count - 1 - i
            low = line.block(i + 1) - keep(i, exact(low), line.face(i + 1), stores)
            high = line.block(j - 1) - keep(j, exact(high), line.face(j), stores)
        sweep = Sweep(count, stores, lambda i: sides[i // mine, i % mine])
        sweep.forward()
        low = low - keep(half, exact(high), line.face(half), stores)
        sweep.back(exact(low), values)
        for e in range(mine):
            out[0, 0, e] = values[place * mine + e]


def on_device(
    right_side,
    old_values,
    element_library,
    wall_library,
    face_library,
    element_index,
    wall_faces,
    face_index,
):
    size = wall_library.shape[1]
    vmem = pl.BlockSpec(memory_space=pltpu.VMEM)
    smem = pl.BlockSpec(memory_space=pltpu.SMEM)
    free = pl.BlockSpec(memory_space=pl.ANY)
    n = lax.axis_size("wall")
    mine = right_side.shape[2]
    count = n * mine
    tail = right_side.shape[3:]
    one = jax.ShapeDtypeStruct(right_side.shape, F32)
    all_sides = jax.ShapeDtypeStruct((n, mine) + tail, F32)
    all_rows = jax.ShapeDtypeStruct((n, 8, 128), jnp.int32)
    stores = [pltpu.VMEM((count, size, size), BF16)] * 4
    fast, sides, index, missed = pl.pallas_call(
        line_kernel,
        out_shape=[one, all_sides, all_rows, jax.ShapeDtypeStruct((8, 128), F32)],
        in_specs=[smem] * 3 + [free] * 5,
        out_specs=[vmem] * 4,
        scratch_shapes=[
            pltpu.VMEM((mine,) + tail, F32),
            pltpu.VMEM(element_library.shape, F32),
            pltpu.VMEM(wall_library.shape, F32),
            pltpu.VMEM(face_library.shape, F32),
            pltpu.VMEM(all_rows.shape, jnp.int32),
            pltpu.VMEM((4, mine) + tail, F32),
            pltpu.VMEM(all_sides.shape, F32),
            pltpu.VMEM((count,) + tail, F32),
            *stores,
            pltpu.SemaphoreType.DMA((4,)),
            pltpu.SemaphoreType.DMA((n - 1,)),
            pltpu.SemaphoreType.DMA((n - 1,)),
            pltpu.SemaphoreType.DMA((4,)),
            pltpu.SemaphoreType.DMA((4,)),
            pltpu.SemaphoreType.DMA((n - 1,)),
            pltpu.SemaphoreType.DMA((n - 1,)),
        ],
        compiler_params=pltpu.CompilerParams(
            vmem_limit_bytes=60 * 1024 * 1024, collective_id=0, has_side_effects=True
        ),
        name="line",
    )(
        element_index, wall_faces, face_index, right_side, old_values,
        element_library, wall_library, face_library,
    )
    return pl.pallas_call(
        check_kernel,
        out_shape=one,
        in_specs=[vmem] * 2 + [free] * 4,
        out_specs=vmem,
        scratch_shapes=[
            pltpu.VMEM(all_sides.shape, F32),
            pltpu.VMEM(all_rows.shape, jnp.int32),
            pltpu.VMEM(element_library.shape, F32),
            pltpu.VMEM(wall_library.shape, F32),
            pltpu.VMEM((count,) + tail, F32),
            pltpu.VMEM((size, size), F32),
            pltpu.VMEM((size, size), F32),
            *stores,
        ],
        compiler_params=pltpu.CompilerParams(vmem_limit_bytes=60 * 1024 * 1024),
        name="check",
    )(missed, fast, sides, index, element_library, wall_library)


def solution(mesh):
    placed = (
        P("span", "stream", "wall", None, None),
        P("span", "stream", "wall", None, None),
        P(),
        P(),
        P(),
        P("span", "stream", "wall"),
        P("span", "stream", "wall", None),
        P("span", "stream", "wall", None),
    )
    return jax.shard_map(
        on_device,
        mesh=mesh,
        in_specs=placed,
        out_specs=P("span", "stream", "wall", None, None),
        check_vma=False,
    )
```

```python
import functools
import jax
import jax.numpy as jnp
from jax import lax
from jax.experimental import pallas as pl
from jax.experimental.pallas import tpu as pltpu
from jax.sharding import PartitionSpec as P

F32 = jnp.float32
BF16 = jnp.bfloat16
LOW_STEPS = 2
CONVERGED = 6e-4
MESH = pl.DeviceIdType.MESH


def dot(a, b, transposed=False):
    dims = (((1,), (1,)), ((), ())) if transposed else (((1,), (0,)), ((), ()))
    return lax.dot_general(a, b, dims, preferred_element_type=F32)


def split(a):
    high = a.astype(BF16)
    return high, (a - high.astype(F32)).astype(BF16)


def dot3(a, b, transposed=False):
    if transposed:
        return dot(a[0], b[0], True) + (dot(a[0], b[1], True) + dot(a[1], b[0], True))
    left = jnp.concatenate([a[0], a[0], a[1]], axis=1)
    return dot(left, jnp.concatenate([b[0], b[1], b[0]], axis=0))


def eye_mask(size):
    row = lax.broadcasted_iota(jnp.int32, (size, size), 0)
    col = lax.broadcasted_iota(jnp.int32, (size, size), 1)
    return row == col


def gauss_jordan(a_ref, x_ref):
    size = a_ref.shape[0]
    x_ref[...] = a_ref[...]

    def step(k, unused):
        current = x_ref[...]
        lanes = lax.broadcasted_iota(jnp.int32, (1, size), 1)
        rows = lax.broadcasted_iota(jnp.int32, (size, 1), 0)
        row = x_ref[pl.ds(k, 1), :]
        pivot = jnp.sum(jnp.where(lanes == k, row, 0.0), axis=1, keepdims=True)
        column = jnp.sum(jnp.where(lanes == k, current, 0.0), axis=1, keepdims=True)
        column = jnp.where(rows == k, 0.0, column)
        scaled = jnp.where(lanes == k, 1.0, row) / pivot
        updated = jnp.where(lanes == k, 0.0, current) - column * scaled
        x_ref[...] = jnp.where(rows == k, scaled, updated)
        return unused

    lax.fori_loop(0, size, step, 0)


def invert(blocks, low_steps=LOW_STEPS):
    size = blocks[0].shape[0]
    mask = eye_mask(size)
    xs = []
    for a in blocks:
        diagonal = jnp.where(mask, a, 0.0)
        row = 1.0 / jnp.sum(diagonal, axis=0, keepdims=True)
        col = 1.0 / jnp.sum(diagonal, axis=1, keepdims=True)
        scaled = a * row * col
        xs.append(jnp.where(mask, 2.0 * row, 0.0) - scaled)
    parts = [split(a) for a in blocks]
    for step in range(low_steps):
        xbs = [x.astype(BF16) for x in xs]
        rs = [jnp.where(mask, 1.0, 0.0) - dot(a[0], xb) for a, xb in zip(parts, xbs)]
        xs = [x + dot(xb, r.astype(BF16)) for x, xb, r in zip(xs, xbs, rs)]
    halves = [split(x) for x in xs]
    rs = [jnp.where(mask, 1.0, 0.0) - dot3(a, x) for a, x in zip(parts, halves)]
    rbs = [r.astype(BF16) for r in rs]
    xs = [x + dot(h[0], rb) for x, h, rb in zip(xs, halves, rbs)]
    missed = jnp.zeros((1, 1), F32)
    for rb in rbs:
        left = dot(rb, rb)
        square = jnp.sum(jnp.sum(left * left, axis=0, keepdims=True), axis=1, keepdims=True)
        missed = missed + jnp.where(square < CONVERGED**2, 0.0, 1.0)
    return xs, missed


class Line:
    def __init__(self, index, mine, library, walls, wide, tall):
        self.library, self.walls, self.wide, self.tall = library, walls, wide, tall
        self.rates, self.faces = [], []
        for owner in range(index.shape[0]):
            rows = index[owner]
            for e in range(mine):
                self.rates.append(rows[e, 0])
                self.faces.append(rows[e, 1])
        self.faces.append(rows[mine - 1, 2])
        self.count = len(self.rates)
        self.size = walls.shape[1]

    def face(self, i):
        return self.walls[self.faces[i]]

    def coupling(self, i):
        return self.wide[self.faces[i]], self.tall[self.faces[i]]

    def block(self, i):
        row = self.library[pl.ds(self.rates[i], 1), :]
        return jnp.where(eye_mask(self.size), row, 0.0) + self.face(i) + self.face(i + 1)


def keep(i, x, coupling, stores):
    wide, tall = coupling
    xs = split(x)
    gs = split(dot(jnp.concatenate([xs[0], xs[0], xs[1]], axis=1), tall))
    for store, value in zip(stores, xs + gs):
        store[i] = value
    return dot(wide, jnp.concatenate([gs[0], gs[1], gs[0]], axis=0))


def widen(walls, wide, tall):
    for k in range(walls.shape[0]):
        high, low = split(walls[k])
        wide[k] = jnp.concatenate([high, high, low], axis=1)
        tall[k] = jnp.concatenate([high, low, high], axis=0)


class Sweep:
    def __init__(self, count, stores, residual):
        self.count, self.half, self.stores, self.residual = count, count // 2, stores, residual

    def pivot(self, i):
        return self.stores[0][i], self.stores[1][i]

    def step(self, i):
        return self.stores[2][i], self.stores[3][i]

    def forward(self):
        count, half, residual = self.count, self.half, self.residual
        carried = [None] * count
        low, high = residual(0), residual(count - 1)
        for i in range(half):
            j = count - 1 - i
            carried[i], carried[j] = split(low), split(high)
            if i + 1 < half:
                low = residual(i + 1) + dot3(carried[i], self.step(i))
                high = residual(j - 1) + dot3(carried[j], self.step(j))
        skip = (half - 1, half)
        self.scaled = {
            i: dot3(carried[i], self.pivot(i)) for i in range(count) if i not in skip
        }
        self.low, self.carried = low, carried[half]

    def back(self, inverse, values):
        count, half = self.count, self.half
        low = self.low + dot3(self.carried, self.step(half))
        middle = dot3(self.carried, self.pivot(half))
        low = dot3(split(low), split(inverse))
        values[half - 1] = low
        lows = split(low)
        high = middle + dot3(lows, self.step(half), True)
        values[half] = high
        highs = split(high)
        for i in range(half - 2, -1, -1):
            j = count - 1 - i
            low = self.scaled[i] + dot3(lows, self.step(i), True)
            high = self.scaled[j] + dot3(highs, self.step(j), True)
            values[i] = low
            values[j] = high
            lows, highs = split(low), split(high)


def line_kernel(
    rates, faces, neighbours, side_in, old, library_in, walls_in, blocks_in,
    out, sides_out, index_out, missed_out,
    side, library, walls, wide, tall, blocks, index, halo, sides, values, ph, plo, gh, glo,
    local_sem, index_send, index_recv, halo_send, halo_recv, side_send, side_recv,
):
    n = lax.axis_size("wall")
    place = lax.axis_index("wall")
    mine = side.shape[0]
    count = n * mine
    half = count // 2
    top = count - 1

    pairs = ((walls_in, walls), (library_in, library), (side_in.at[0, 0], side), (blocks_in, blocks))
    loads = [
        pltpu.make_async_copy(src, dst, local_sem.at[k]) for k, (src, dst) in enumerate(pairs)
    ]
    for load in loads:
        load.start()

    row = lax.broadcasted_iota(jnp.int32, index.shape[1:], 0)
    col = lax.broadcasted_iota(jnp.int32, index.shape[1:], 1)
    own = jnp.zeros(index.shape[1:], jnp.int32)
    for e in range(mine):
        for c, value in enumerate((rates[0, 0, e], faces[0, 0, e, 0], faces[0, 0, e, 1])):
            own = jnp.where(jnp.logical_and(row == e, col == c), value, own)
    index[place] = own

    partners = [{"wall": lax.rem(place + s, n)} for s in range(1, n)]
    beside = []
    for base, axis in ((0, "span"), (2, "stream")):
        m = lax.axis_size(axis)
        here = lax.axis_index(axis)
        beside.append((base, {axis: lax.rem(here + 1, m)}))
        if m > 2:
            beside.append((base + 1, {axis: lax.rem(here + m - 1, m)}))
    barrier = pltpu.get_barrier_semaphore()
    for target in partners + [target for unused, target in beside]:
        pl.semaphore_signal(barrier, inc=1, device_id=target, device_id_type=MESH)
    pl.semaphore_wait(barrier, len(partners) + len(beside))

    def spread(buffer, send, recv):
        copies = [
            pltpu.make_async_remote_copy(
                src_ref=buffer.at[place],
                dst_ref=buffer.at[place],
                send_sem=send.at[k],
                recv_sem=recv.at[k],
                device_id=target,
                device_id_type=MESH,
            )
            for k, target in enumerate(partners)
        ]
        for copy in copies:
            copy.start()
        return copies

    index_copies = spread(index, index_send, index_recv)
    halo_copies = [
        pltpu.make_async_remote_copy(
            src_ref=old.at[0, 0],
            dst_ref=halo.at[k],
            send_sem=halo_send.at[k],
            recv_sem=halo_recv.at[k],
            device_id=target,
            device_id_type=MESH,
        )
        for k, target in beside
    ]
    for copy in halo_copies:
        copy.start()
    for load in loads[:2]:
        load.wait()
    widen(walls, wide, tall)
    for copy in index_copies:
        copy.wait()
    line = Line(index, mine, library, walls, wide, tall)
    stores = (ph, plo, gh, glo)
    low, high = line.block(0), line.block(top)
    missed = jnp.zeros((1, 1), F32)
    side_copies = None
    for i in range(half - 1):
        j = top - i
        (x, y), off = invert([low, high])
        missed = missed + off
        low = line.block(i + 1) - keep(i, x, line.coupling(i + 1), stores)
        high = line.block(j - 1) - keep(j, y, line.coupling(j), stores)
        if i == max(0, half - 3):
            for load in loads[2:]:
                load.wait()
            for copy in halo_copies:
                copy.wait()
            arrived = [k for k, unused in beside]
            for e in range(mine):
                total = side[e]
                for d in range(4):
                    near = halo[d if d in arrived else d - 1, e]
                    block = blocks[neighbours[0, 0, e, d]]
                    total = total - dot3(split(near), split(block), True)
                sides[place, e] = total
            side_copies = spread(sides, side_send, side_recv)
    for copy in side_copies:
        copy.wait()
    handed = [
        pltpu.make_async_copy(sides, sides_out, local_sem.at[4]),
        pltpu.make_async_copy(index, index_out, local_sem.at[5]),
    ]
    for copy in handed:
        copy.start()
    sweep = Sweep(count, stores, lambda i: sides[i // mine, i % mine])
    sweep.forward()
    (y,), off = invert([high])
    missed = missed + off
    low = low - keep(half, y, line.coupling(half), stores)
    (x,), off = invert([low], 1)
    missed = missed + off
    sweep.back(x, values)
    for e in range(mine):
        out[0, 0, e] = values[place * mine + e]
    for copy in handed:
        copy.wait()
    missed_out[...] = jnp.broadcast_to(missed, missed_out.shape)


def check_kernel(
    missed, fast, sides_in, index_in, library_in, walls_in,
    out, sides, index, library, walls, wide, tall, values, block, inverse, ph, plo, gh, glo,
):
    out[...] = fast[...]

    @pl.when(jnp.logical_not(missed[0:1, 0:1][0, 0] < 0.5))
    def _():
        for src, dst in (
            (sides_in, sides), (index_in, index), (library_in, library), (walls_in, walls)
        ):
            pltpu.sync_copy(src, dst)
        n, mine = sides.shape[:2]
        count = n * mine
        half = count // 2
        place = lax.axis_index("wall")
        widen(walls, wide, tall)
        line = Line(index, mine, library, walls, wide, tall)
        stores = (ph, plo, gh, glo)

        def exact(a):
            block[...] = a
            gauss_jordan(block, inverse)
            return inverse[...]

        low = line.block(0)
        high = line.block(count - 1)
        for i in range(half - 1):
            j = count - 1 - i
            low = line.block(i + 1) - keep(i, exact(low), line.coupling(i + 1), stores)
            high = line.block(j - 1) - keep(j, exact(high), line.coupling(j), stores)
        sweep = Sweep(count, stores, lambda i: sides[i // mine, i % mine])
        sweep.forward()
        low = low - keep(half, exact(high), line.coupling(half), stores)
        sweep.back(exact(low), values)
        for e in range(mine):
            out[0, 0, e] = values[place * mine + e]


def on_device(
    right_side,
    old_values,
    element_library,
    wall_library,
    face_library,
    element_index,
    wall_faces,
    face_index,
):
    size = wall_library.shape[1]
    vmem = pl.BlockSpec(memory_space=pltpu.VMEM)
    smem = pl.BlockSpec(memory_space=pltpu.SMEM)
    free = pl.BlockSpec(memory_space=pl.ANY)
    n = lax.axis_size("wall")
    mine = right_side.shape[2]
    count = n * mine
    tail = right_side.shape[3:]
    one = jax.ShapeDtypeStruct(right_side.shape, F32)
    all_sides = jax.ShapeDtypeStruct((n, mine) + tail, F32)
    all_rows = jax.ShapeDtypeStruct((n, 8, 128), jnp.int32)
    stores = [pltpu.VMEM((count, size, size), BF16)] * 4
    fast, sides, index, missed = pl.pallas_call(
        line_kernel,
        out_shape=[one, all_sides, all_rows, jax.ShapeDtypeStruct((8, 128), F32)],
        in_specs=[smem] * 3 + [free] * 5,
        out_specs=[vmem, free, free, vmem],
        scratch_shapes=[
            pltpu.VMEM((mine,) + tail, F32),
            pltpu.VMEM(element_library.shape, F32),
            pltpu.VMEM(wall_library.shape, F32),
            pltpu.VMEM((wall_library.shape[0], size, 3 * size), BF16),
            pltpu.VMEM((wall_library.shape[0], 3 * size, size), BF16),
            pltpu.VMEM(face_library.shape, F32),
            pltpu.VMEM(all_rows.shape, jnp.int32),
            pltpu.VMEM((4, mine) + tail, F32),
            pltpu.VMEM(all_sides.shape, F32),
            pltpu.VMEM((count,) + tail, F32),
            *stores,
            pltpu.SemaphoreType.DMA((6,)),
            pltpu.SemaphoreType.DMA((n - 1,)),
            pltpu.SemaphoreType.DMA((n - 1,)),
            pltpu.SemaphoreType.DMA((4,)),
            pltpu.SemaphoreType.DMA((4,)),
            pltpu.SemaphoreType.DMA((n - 1,)),
            pltpu.SemaphoreType.DMA((n - 1,)),
        ],
        compiler_params=pltpu.CompilerParams(
            vmem_limit_bytes=60 * 1024 * 1024, collective_id=0, has_side_effects=True
        ),
        name="line",
    )(
        element_index, wall_faces, face_index, right_side, old_values,
        element_library, wall_library, face_library,
    )
    return pl.pallas_call(
        check_kernel,
        out_shape=one,
        in_specs=[vmem] * 2 + [free] * 4,
        out_specs=vmem,
        scratch_shapes=[
            pltpu.VMEM(all_sides.shape, F32),
            pltpu.VMEM(all_rows.shape, jnp.int32),
            pltpu.VMEM(element_library.shape, F32),
            pltpu.VMEM(wall_library.shape, F32),
            pltpu.VMEM((wall_library.shape[0], size, 3 * size), BF16),
            pltpu.VMEM((wall_library.shape[0], 3 * size, size), BF16),
            pltpu.VMEM((count,) + tail, F32),
            pltpu.VMEM((size, size), F32),
            pltpu.VMEM((size, size), F32),
            *stores,
        ],
        compiler_params=pltpu.CompilerParams(vmem_limit_bytes=60 * 1024 * 1024),
        name="check",
    )(missed, fast, sides, index, element_library, wall_library)


def solution(mesh):
    placed = (
        P("span", "stream", "wall", None, None),
        P("span", "stream", "wall", None, None),
        P(),
        P(),
        P(),
        P("span", "stream", "wall"),
        P("span", "stream", "wall", None),
        P("span", "stream", "wall", None),
    )
    return jax.shard_map(
        on_device,
        mesh=mesh,
        in_specs=placed,
        out_specs=P("span", "stream", "wall", None, None),
        check_vma=False,
    )
```

```python
import functools
import jax
import jax.numpy as jnp
from jax import lax
from jax.experimental import pallas as pl
from jax.experimental.pallas import tpu as pltpu
from jax.sharding import PartitionSpec as P

F32 = jnp.float32
BF16 = jnp.bfloat16
LOW_STEPS = 2
CONVERGED = 6e-4
MESH = pl.DeviceIdType.MESH


def dot(a, b, transposed=False):
    dims = (((1,), (1,)), ((), ())) if transposed else (((1,), (0,)), ((), ()))
    return lax.dot_general(a, b, dims, preferred_element_type=F32)


def split(a):
    high = a.astype(BF16)
    return high, (a - high.astype(F32)).astype(BF16)


def dot3(a, b, transposed=False):
    if transposed:
        return dot(a[0], b[0], True) + (dot(a[0], b[1], True) + dot(a[1], b[0], True))
    left = jnp.concatenate([a[0], a[0], a[1]], axis=1)
    return dot(left, jnp.concatenate([b[0], b[1], b[0]], axis=0))


def eye_mask(size):
    row = lax.broadcasted_iota(jnp.int32, (size, size), 0)
    col = lax.broadcasted_iota(jnp.int32, (size, size), 1)
    return row == col


def gauss_jordan(a_ref, x_ref):
    size = a_ref.shape[0]
    x_ref[...] = a_ref[...]

    def step(k, unused):
        current = x_ref[...]
        lanes = lax.broadcasted_iota(jnp.int32, (1, size), 1)
        rows = lax.broadcasted_iota(jnp.int32, (size, 1), 0)
        row = x_ref[pl.ds(k, 1), :]
        pivot = jnp.sum(jnp.where(lanes == k, row, 0.0), axis=1, keepdims=True)
        column = jnp.sum(jnp.where(lanes == k, current, 0.0), axis=1, keepdims=True)
        column = jnp.where(rows == k, 0.0, column)
        scaled = jnp.where(lanes == k, 1.0, row) / pivot
        updated = jnp.where(lanes == k, 0.0, current) - column * scaled
        x_ref[...] = jnp.where(rows == k, scaled, updated)
        return unused

    lax.fori_loop(0, size, step, 0)


def invert(blocks, low_steps=LOW_STEPS):
    size = blocks[0].shape[0]
    mask = eye_mask(size)
    xs = []
    for a in blocks:
        diagonal = jnp.where(mask, a, 0.0)
        row = 1.0 / jnp.sum(diagonal, axis=0, keepdims=True)
        col = 1.0 / jnp.sum(diagonal, axis=1, keepdims=True)
        scaled = a * row * col
        xs.append(jnp.where(mask, 2.0 * row, 0.0) - scaled)
    parts = [split(a) for a in blocks]
    for step in range(low_steps):
        xbs = [x.astype(BF16) for x in xs]
        rs = [jnp.where(mask, 1.0, 0.0) - dot(a[0], xb) for a, xb in zip(parts, xbs)]
        xs = [x + dot(xb, r.astype(BF16)) for x, xb, r in zip(xs, xbs, rs)]
    halves = [split(x) for x in xs]
    rs = [jnp.where(mask, 1.0, 0.0) - dot3(a, x) for a, x in zip(parts, halves)]
    rbs = [r.astype(BF16) for r in rs]
    xs = [x + dot(h[0], rb) for x, h, rb in zip(xs, halves, rbs)]
    missed = jnp.zeros((1, 1), F32)
    for rb in rbs:
        left = dot(rb, rb)
        square = jnp.sum(jnp.sum(left * left, axis=0, keepdims=True), axis=1, keepdims=True)
        missed = missed + jnp.where(square < CONVERGED**2, 0.0, 1.0)
    return xs, missed


class Line:
    def __init__(self, index, mine, library, walls, wide, tall):
        self.library, self.walls, self.wide, self.tall = library, walls, wide, tall
        self.rates, self.faces = [], []
        for owner in range(index.shape[0]):
            rows = index[owner]
            for e in range(mine):
                self.rates.append(rows[e, 0])
                self.faces.append(rows[e, 1])
        self.faces.append(rows[mine - 1, 2])
        self.count = len(self.rates)
        self.size = walls.shape[1]

    def face(self, i):
        return self.walls[self.faces[i]]

    def coupling(self, i):
        return self.wide[self.faces[i]], self.tall[self.faces[i]]

    def block(self, i):
        row = self.library[pl.ds(self.rates[i], 1), :]
        return jnp.where(eye_mask(self.size), row, 0.0) + self.face(i) + self.face(i + 1)


def keep(i, x, coupling, stores):
    wide, tall = coupling
    xs = split(x)
    gs = split(dot(jnp.concatenate([xs[0], xs[0], xs[1]], axis=1), tall))
    for store, value in zip(stores, xs + gs):
        store[i] = value
    return dot(wide, jnp.concatenate([gs[0], gs[1], gs[0]], axis=0))


def widen(walls, wide, tall):
    for k in range(walls.shape[0]):
        high, low = split(walls[k])
        wide[k] = jnp.concatenate([high, high, low], axis=1)
        tall[k] = jnp.concatenate([high, low, high], axis=0)


class Sweep:
    def __init__(self, count, stores, residual):
        self.count, self.half, self.stores, self.residual = count, count // 2, stores, residual

    def pivot(self, i):
        return self.stores[0][i], self.stores[1][i]

    def step(self, i):
        return self.stores[2][i], self.stores[3][i]

    def forward(self):
        count, half, residual = self.count, self.half, self.residual
        carried = [None] * count
        low, high = residual(0), residual(count - 1)
        for i in range(half):
            j = count - 1 - i
            carried[i], carried[j] = split(low), split(high)
            if i + 1 < half:
                low = residual(i + 1) + dot3(carried[i], self.step(i))
                high = residual(j - 1) + dot3(carried[j], self.step(j))
        skip = (half - 1, half)
        self.scaled = {
            i: dot3(carried[i], self.pivot(i)) for i in range(count) if i not in skip
        }
        self.low, self.carried = low, carried[half]

    def back(self, inverse, values):
        count, half = self.count, self.half
        low = self.low + dot3(self.carried, self.step(half))
        middle = dot3(self.carried, self.pivot(half))
        low = dot3(split(low), split(inverse))
        values[half - 1] = low
        lows = split(low)
        high = middle + dot3(lows, self.step(half), True)
        values[half] = high
        highs = split(high)
        for i in range(half - 2, -1, -1):
            j = count - 1 - i
            low = self.scaled[i] + dot3(lows, self.step(i), True)
            high = self.scaled[j] + dot3(highs, self.step(j), True)
            values[i] = low
            values[j] = high
            lows, highs = split(low), split(high)


def line_kernel(
    rates, faces, neighbours, side_in, old, library_in, walls_in, blocks_in,
    out, sides_out, index_out, missed_out,
    side, library, walls, wide, tall, blocks, index, halo, sides, values, ph, plo, gh, glo,
    local_sem, index_send, index_recv, halo_send, halo_recv, side_send, side_recv,
):
    n = lax.axis_size("wall")
    place = lax.axis_index("wall")
    mine = side.shape[0]
    count = n * mine
    half = count // 2
    top = count - 1

    pairs = ((walls_in, walls), (library_in, library), (side_in.at[0, 0], side), (blocks_in, blocks))
    loads = [
        pltpu.make_async_copy(src, dst, local_sem.at[k]) for k, (src, dst) in enumerate(pairs)
    ]
    for load in loads:
        load.start()

    row = lax.broadcasted_iota(jnp.int32, index.shape[1:], 0)
    col = lax.broadcasted_iota(jnp.int32, index.shape[1:], 1)
    own = jnp.zeros(index.shape[1:], jnp.int32)
    for e in range(mine):
        for c, value in enumerate((rates[0, 0, e], faces[0, 0, e, 0], faces[0, 0, e, 1])):
            own = jnp.where(jnp.logical_and(row == e, col == c), value, own)
    index[place] = own

    partners = [{"wall": lax.rem(place + s, n)} for s in range(1, n)]
    beside = []
    for base, axis in ((0, "span"), (2, "stream")):
        m = lax.axis_size(axis)
        here = lax.axis_index(axis)
        beside.append((base, {axis: lax.rem(here + 1, m)}))
        if m > 2:
            beside.append((base + 1, {axis: lax.rem(here + m - 1, m)}))
    barrier = pltpu.get_barrier_semaphore()
    for target in partners + [target for unused, target in beside]:
        pl.semaphore_signal(barrier, inc=1, device_id=target, device_id_type=MESH)
    pl.semaphore_wait(barrier, len(partners) + len(beside))

    def spread(buffer, send, recv):
        copies = [
            pltpu.make_async_remote_copy(
                src_ref=buffer.at[place],
                dst_ref=buffer.at[place],
                send_sem=send.at[k],
                recv_sem=recv.at[k],
                device_id=target,
                device_id_type=MESH,
            )
            for k, target in enumerate(partners)
        ]
        for copy in copies:
            copy.start()
        return copies

    index_copies = spread(index, index_send, index_recv)
    halo_copies = [
        pltpu.make_async_remote_copy(
            src_ref=old.at[0, 0],
            dst_ref=halo.at[k],
            send_sem=halo_send.at[k],
            recv_sem=halo_recv.at[k],
            device_id=target,
            device_id_type=MESH,
        )
        for k, target in beside
    ]
    for copy in halo_copies:
        copy.start()
    for load in loads[:2]:
        load.wait()
    widen(walls, wide, tall)
    for copy in index_copies:
        copy.wait()
    line = Line(index, mine, library, walls, wide, tall)
    stores = (ph, plo, gh, glo)
    low, high = line.block(0), line.block(top)
    missed = jnp.zeros((1, 1), F32)
    side_copies = None
    for i in range(half - 1):
        j = top - i
        (x, y), off = invert([low, high])
        missed = missed + off
        low = line.block(i + 1) - keep(i, x, line.coupling(i + 1), stores)
        high = line.block(j - 1) - keep(j, y, line.coupling(j), stores)
        if i == max(0, half - 3):
            for load in loads[2:]:
                load.wait()
            for copy in halo_copies:
                copy.wait()
            arrived = [k for k, unused in beside]
            for e in range(mine):
                total = side[e]
                for d in range(4):
                    near = halo[d if d in arrived else d - 1, e]
                    block = blocks[neighbours[0, 0, e, d]]
                    total = total - dot3(split(near), split(block), True)
                sides[place, e] = total
            side_copies = spread(sides, side_send, side_recv)
    for copy in side_copies:
        copy.wait()
    handed = [
        pltpu.make_async_copy(sides, sides_out, local_sem.at[4]),
        pltpu.make_async_copy(index, index_out, local_sem.at[5]),
    ]
    for copy in handed:
        copy.start()
    sweep = Sweep(count, stores, lambda i: sides[i // mine, i % mine])
    sweep.forward()
    (y,), off = invert([high])
    missed = missed + off
    low = low - keep(half, y, line.coupling(half), stores)
    (x,), off = invert([low], 1)
    missed = missed + off
    sweep.back(x, values)
    for e in range(mine):
        out[0, 0, e] = values[place * mine + e]
    for copy in handed:
        copy.wait()
    missed_out[...] = jnp.broadcast_to(missed, missed_out.shape)


def check_kernel(
    missed, fast, sides_in, index_in, library_in, walls_in,
    out, sides, index, library, walls, wide, tall, values, block, inverse, ph, plo, gh, glo, sem,
):
    passed = [
        pltpu.make_async_copy(fast.at[0, 0, e], out.at[0, 0, e], sem.at[e])
        for e in range(sides.shape[1])
    ]
    for copy in passed:
        copy.start()
    for copy in passed:
        copy.wait()

    @pl.when(jnp.logical_not(missed[0:1, 0:1][0, 0] < 0.5))
    def _():
        for src, dst in (
            (sides_in, sides), (index_in, index), (library_in, library), (walls_in, walls)
        ):
            pltpu.sync_copy(src, dst)
        n, mine = sides.shape[:2]
        count = n * mine
        half = count // 2
        place = lax.axis_index("wall")
        widen(walls, wide, tall)
        line = Line(index, mine, library, walls, wide, tall)
        stores = (ph, plo, gh, glo)

        def exact(a):
            block[...] = a
            gauss_jordan(block, inverse)
            return inverse[...]

        low = line.block(0)
        high = line.block(count - 1)
        for i in range(half - 1):
            j = count - 1 - i
            low = line.block(i + 1) - keep(i, exact(low), line.coupling(i + 1), stores)
            high = line.block(j - 1) - keep(j, exact(high), line.coupling(j), stores)
        sweep = Sweep(count, stores, lambda i: sides[i // mine, i % mine])
        sweep.forward()
        low = low - keep(half, exact(high), line.coupling(half), stores)
        sweep.back(exact(low), values)
        for e in range(mine):
            pltpu.sync_copy(values.at[place * mine + e], out.at[0, 0, e])


def on_device(
    right_side,
    old_values,
    element_library,
    wall_library,
    face_library,
    element_index,
    wall_faces,
    face_index,
):
    size = wall_library.shape[1]
    vmem = pl.BlockSpec(memory_space=pltpu.VMEM)
    smem = pl.BlockSpec(memory_space=pltpu.SMEM)
    free = pl.BlockSpec(memory_space=pl.ANY)
    n = lax.axis_size("wall")
    mine = right_side.shape[2]
    count = n * mine
    tail = right_side.shape[3:]
    one = jax.ShapeDtypeStruct(right_side.shape, F32)
    all_sides = jax.ShapeDtypeStruct((n, mine) + tail, F32)
    all_rows = jax.ShapeDtypeStruct((n, 8, 128), jnp.int32)
    stores = [pltpu.VMEM((count, size, size), BF16)] * 4
    fast, sides, index, missed = pl.pallas_call(
        line_kernel,
        out_shape=[one, all_sides, all_rows, jax.ShapeDtypeStruct((8, 128), F32)],
        in_specs=[smem] * 3 + [free] * 5,
        out_specs=[vmem, free, free, vmem],
        scratch_shapes=[
            pltpu.VMEM((mine,) + tail, F32),
            pltpu.VMEM(element_library.shape, F32),
            pltpu.VMEM(wall_library.shape, F32),
            pltpu.VMEM((wall_library.shape[0], size, 3 * size), BF16),
            pltpu.VMEM((wall_library.shape[0], 3 * size, size), BF16),
            pltpu.VMEM(face_library.shape, F32),
            pltpu.VMEM(all_rows.shape, jnp.int32),
            pltpu.VMEM((4, mine) + tail, F32),
            pltpu.VMEM(all_sides.shape, F32),
            pltpu.VMEM((count,) + tail, F32),
            *stores,
            pltpu.SemaphoreType.DMA((6,)),
            pltpu.SemaphoreType.DMA((n - 1,)),
            pltpu.SemaphoreType.DMA((n - 1,)),
            pltpu.SemaphoreType.DMA((4,)),
            pltpu.SemaphoreType.DMA((4,)),
            pltpu.SemaphoreType.DMA((n - 1,)),
            pltpu.SemaphoreType.DMA((n - 1,)),
        ],
        compiler_params=pltpu.CompilerParams(
            vmem_limit_bytes=60 * 1024 * 1024, collective_id=0, has_side_effects=True
        ),
        name="line",
    )(
        element_index, wall_faces, face_index, right_side, old_values,
        element_library, wall_library, face_library,
    )
    return pl.pallas_call(
        check_kernel,
        out_shape=one,
        in_specs=[vmem] + [free] * 5,
        out_specs=free,
        scratch_shapes=[
            pltpu.VMEM(all_sides.shape, F32),
            pltpu.VMEM(all_rows.shape, jnp.int32),
            pltpu.VMEM(element_library.shape, F32),
            pltpu.VMEM(wall_library.shape, F32),
            pltpu.VMEM((wall_library.shape[0], size, 3 * size), BF16),
            pltpu.VMEM((wall_library.shape[0], 3 * size, size), BF16),
            pltpu.VMEM((count,) + tail, F32),
            pltpu.VMEM((size, size), F32),
            pltpu.VMEM((size, size), F32),
            *stores,
            pltpu.SemaphoreType.DMA((mine,)),
        ],
        compiler_params=pltpu.CompilerParams(vmem_limit_bytes=60 * 1024 * 1024),
        name="check",
    )(missed, fast, sides, index, element_library, wall_library)


def solution(mesh):
    placed = (
        P("span", "stream", "wall", None, None),
        P("span", "stream", "wall", None, None),
        P(),
        P(),
        P(),
        P("span", "stream", "wall"),
        P("span", "stream", "wall", None),
        P("span", "stream", "wall", None),
    )
    return jax.shard_map(
        on_device,
        mesh=mesh,
        in_specs=placed,
        out_specs=P("span", "stream", "wall", None, None),
        check_vma=False,
    )
```
